32 devices in a mesh: col: 8 (over y, x, core), row: 4 (over z).
Axes of the slice: x: 2, y: 2, z: 4, core: 2. Of those that a mesh axis runs over, the one named last changes fastest.
Arguments:
- normal_matrix: float32 [4, 4, 128, 2, 8, 128], P(None, 'row', None, None, 'col'), may hold values from -3 to 5.5, as said below
- right_sides: float32 [64, 4, 4, 128], P('col', None, 'row'), may hold values from -6 to 6
Outputs:
- reduced_matrix: float32 [4, 4, 128, 2, 8, 128], P(None, 'row', None, None, 'col')
- reduced_sides: float32 [64, 4, 4, 128], P('col', None, 'row')
The draws below stay inside these ranges and needn't reach their ends.
Inputs may be any that keep to these rules, and one draw needn't show every extreme that they name: `normal_matrix`: A is symmetric; its leading 128 x 128 block is strictly diagonally dominant with a positive diagonal.
All inputs are finite; a program needn't handle non-finite values.
Results may differ from the reference program's by a relative error of at most 0.00005.
Values sent between devices are 32-bit elements; how exact they have to be, the bound alone decides.
A program may use at most 64 MiB of HBM per device.

```python
import jax
import jax.numpy as jnp
from jax import lax

NB = 128
CB = 2
ROW_DEVS = 4
COL_DEVS = 8
RB = 4
M = 2048
R = 64


def draw_normal_matrix(key, part):
    first_key, second_key, third_key = jax.random.split(key, 3)
    size_total = CB * COL_DEVS * NB
    base = jnp.clip(jax.random.normal(first_key, (size_total, size_total), jnp.float32), -4.0, 4.0)
    offset = 0.3
    full = 0.5 * (base + base.T) * 0.70710678
    offdiag = jax.random.uniform(second_key, (NB, NB), jnp.float32, -1.0, 1.0)
    offdiag = (0.5 * (offdiag + offdiag.T) + offset) * (2.0 / NB)
    diagonal = 3.5 + 2.0 * jax.random.uniform(third_key, (NB,), jnp.float32)
    eye = jnp.eye(NB, dtype=jnp.float32)
    corner = offdiag * (1.0 - eye) + eye * diagonal[:, None]
    full = full.at[:NB, :NB].set(corner)
    return full.reshape(RB, ROW_DEVS, NB, CB, COL_DEVS, NB)


def steps_of(key, dims, cuts, low, high):
    gain = 1.0
    for dim, blocks in cuts:
        steps = jax.random.uniform(jax.random.fold_in(jax.random.fold_in(key, 6), dim), (blocks,), jnp.float32, low / len(cuts), high / len(cuts))
        gain = gain * jnp.repeat(jnp.exp(steps), dims[dim] // blocks).reshape((-1,) + (1,) * (len(dims) - 1 - dim))
    return gain


def noise(rng, dims, scale, reach, cuts=(), held_as=jnp.bfloat16):
    gain = steps_of(rng, dims, cuts, -0.22, 0.18) if cuts else 1.0
    values = jax.random.normal(rng, dims, jnp.float32) * scale * gain
    return jnp.minimum(jnp.maximum(values, -reach), reach).astype(held_as)


def setup_inputs(seed: int = 0) -> dict:
    key_list = jax.random.split(jax.random.key(seed), 3)
    normal_matrix = draw_normal_matrix(jax.random.fold_in(key_list[2], 71), 0)
    right_sides = noise(key_list[1], (R, RB, ROW_DEVS, NB), 1.0, 6.0, ((0, 8), (2, 4)), jnp.float32)
    return dict(normal_matrix=normal_matrix, right_sides=right_sides)


def reference(normal_matrix, right_sides):
    full = normal_matrix.reshape(M, M)
    corner = jnp.linalg.cholesky(full[:NB, :NB])
    panel = jax.scipy.linalg.solve_triangular(corner, full[:, :NB].T, lower=True).T
    change = jnp.dot(panel.astype(jnp.float32), panel.T.astype(jnp.float32), precision=lax.Precision.HIGHEST, preferred_element_type=jnp.float32)
    trailing = full - change
    ids = jnp.arange(M)
    inner = (ids[:, None] >= NB) & (ids[None, :] >= NB)
    result = jnp.where(inner, trailing, jnp.float32(0.0))
    column = panel.at[:NB].set(corner)
    result = result.at[:, :NB].set(column)
    sides = right_sides.reshape(R, M)
    lead = jax.scipy.linalg.solve_triangular(corner, sides[:, :NB].T, lower=True).T
    reduced = sides - jnp.dot(lead.astype(jnp.float32), panel.T.astype(jnp.float32), precision=lax.Precision.HIGHEST, preferred_element_type=jnp.float32)
    reduced = reduced.at[:, :NB].set(lead)
    return (result.reshape(normal_matrix.shape), reduced.reshape(right_sides.shape))
```

```python
import functools

import jax
import jax.numpy as jnp
from jax import lax
from jax.experimental import pallas as pl
from jax.experimental.pallas import tpu as pltpu
from jax.sharding import PartitionSpec as P

F32 = jnp.float32


def dot(a, b, dims):
    return lax.dot_general(
        a, b, (dims, ((), ())), precision=lax.Precision.HIGHEST, preferred_element_type=F32
    )


def eliminate(first, second):
    count = len(first)
    shape = first[0].shape
    sub = lax.broadcasted_iota(jnp.int32, shape, 0)
    first, second = list(first), list(second)
    for b in range(count):
        cols = [
            [jnp.broadcast_to(first[t][:, 8 * b + i : 8 * b + i + 1], shape) for i in range(8)]
            for t in range(b, count)
        ]
        e = [[None] * 8 for _ in range(8)]
        for i in range(8):
            for j in range(i + 1):
                e[j][i] = jnp.broadcast_to(cols[0][i][j : j + 1, :], shape)
        rows1 = [jnp.broadcast_to(first[b][j : j + 1, :], shape) for j in range(8)]
        rows2 = [jnp.broadcast_to(second[b][j : j + 1, :], shape) for j in range(8)]
        for k in range(8):
            scale = lax.rsqrt(e[k][k])
            low = {j: e[k][j] * scale for j in range(k + 1, 8)}
            for i in range(k + 1, 8):
                for j in range(k + 1, i + 1):
                    e[j][i] = e[j][i] - low[j] * low[i]
            rows1[k] = rows1[k] * scale
            rows2[k] = rows2[k] * scale
            for j in range(k + 1, 8):
                rows1[j] = rows1[j] - low[j] * rows1[k]
                rows2[j] = rows2[j] - low[j] * rows2[k]
            for t in range(b + 1, count):
                c = cols[t - b]
                c[k] = c[k] * scale
                for j in range(k + 1, 8):
                    c[j] = c[j] - low[j] * c[k]
                first[t] = first[t] - c[k] * rows1[k]
                second[t] = second[t] - c[k] * rows2[k]
        done1, done2 = rows1[0], rows2[0]
        for k in range(1, 8):
            done1 = jnp.where(sub == k, rows1[k], done1)
            done2 = jnp.where(sub == k, rows2[k], done2)
        first[b], second[b] = done1, done2
    return jnp.concatenate(first, axis=0), jnp.concatenate(second, axis=0)


def groups(x):
    return [x[8 * t : 8 * t + 8] for t in range(x.shape[0] // 8)]


def kernel(
    sizes, a_ref, b_ref, out_ref, red_ref,
    ybuf, zbuf, tbuf, wbuf, ubuf,
    ysend, yrecv, zsend, zrecv, wrow, wcol, wrecv,
):
    row_count, col_count, rb, cb, nb, sides = sizes
    half = nb // 2
    r = lax.axis_index("row")
    c = lax.axis_index("col")
    bits = max(1, (col_count - 1).bit_length())
    root = (r == 0) & (c == 0)
    sends_down = [
        (lax.rem(c, 2 ** (b + 1)) == 0) & (c + 2**b < col_count) for b in range(bits)
    ]
    parent = c * 0
    for b in range(bits):
        parent = jnp.where(lax.rem(c, 2 ** (b + 1)) == 2**b, c - 2**b, parent)

    @pl.when(c == 0)
    def _():
        for i in range(rb):
            ybuf[i] = a_ref[pl.ds(i * nb * cb, nb, stride=cb), :]

    @pl.when(r == 0)
    def _():
        for j in range(cb):
            zbuf[j] = a_ref[pl.ds(j, nb, stride=cb), :]
        tbuf[...] = b_ref[pl.ds(0, sides, stride=rb), :]

    barrier = pltpu.get_barrier_semaphore()

    def greet(row, col):
        pl.semaphore_signal(
            barrier, inc=1, device_id={"row": row, "col": col}, device_id_type=pl.DeviceIdType.MESH
        )

    @pl.when(c != 0)
    def _():
        greet(r, parent)
        greet(r, 0)

    @pl.when(r != 0)
    def _():
        greet(r - 1, c)

    @pl.when((r != 0) & (c == 0))
    def _():
        greet(0, 0)

    targets = jnp.where(r < row_count - 1, 1, 0)
    for b in range(bits):
        targets = targets + jnp.where(sends_down[b], 1, 0)
    targets = targets + jnp.where(c == 0, col_count - 1, 0)
    targets = targets + jnp.where(root, row_count - 1, 0)

    @pl.when(targets > 0)
    def _():
        pl.semaphore_wait(barrier, targets)

    def copy(ref, send, recv, row, col):
        return pltpu.make_async_remote_copy(
            src_ref=ref,
            dst_ref=ref,
            send_sem=send,
            recv_sem=recv,
            device_id={"row": row, "col": col},
            device_id_type=pl.DeviceIdType.MESH,
        )

    def y_copy(i, b):
        return copy(ybuf.at[i], ysend.at[b, i], yrecv.at[i], r, c + 2**b)

    def z_copy(j):
        ref = zbuf.at[j] if j < cb else tbuf
        return copy(ref, zsend.at[j], zrecv.at[j], r + 1, c)

    def w_row(p, row):
        return copy(wbuf.at[p], wrow.at[row, p], wrecv.at[p], row, 0)

    def w_col(p, col):
        return copy(wbuf.at[p], wcol.at[col, p], wrecv.at[p], r, col)

    for i in range(max(rb, cb + 1)):
        if i < rb:
            @pl.when(c != 0)
            def _(i=i):
                y_copy(i, 0).wait_recv()

            for b in reversed(range(bits)):
                @pl.when(sends_down[b])
                def _(i=i, b=b):
                    y_copy(i, b).start()

        if i <= cb:
            @pl.when(r != 0)
            def _(i=i):
                z_copy(i).wait_recv()

            @pl.when(r < row_count - 1)
            def _(i=i):
                z_copy(i).start()

    def spread(p):
        for col in reversed(range(1, col_count)):
            w_col(p, col).start()

    @pl.when(root)
    def _():
        lane = lax.broadcasted_iota(jnp.int32, (half, nb), 1)
        sub = lax.broadcasted_iota(jnp.int32, (half, nb), 0)
        right = jnp.where(lane == sub + half, 1.0, 0.0).astype(F32)
        up, inv = eliminate(groups(ybuf[0, 0:half, :]), groups(right))
        wbuf[0] = pltpu.roll(inv, half, 1)
        ubuf[0] = up
        for row in reversed(range(1, row_count)):
            w_row(0, row).start()
        spread(0)
        up12 = pltpu.roll(up, half, 1)
        beside = jnp.where(lane < half, up12, inv)
        change = dot(up12, beside, ((0,), (0,)))[0:half, :]
        low_rows = pltpu.roll(ybuf[0, half:nb, :], half, 1)
        start = jnp.where(lane < half, low_rows, 0.0) - change
        up, inv = eliminate(groups(start), groups(right))
        wbuf[1] = jnp.where(lane < half, pltpu.roll(up, half, 1), inv)
        ubuf[1] = jnp.where(lane < half, 0.0, pltpu.roll(up, half, 1))
        for row in reversed(range(1, row_count)):
            w_row(1, row).start()
        spread(1)

    @pl.when((c == 0) & (r != 0))
    def _():
        for p in range(2):
            w_row(p, 0).wait_recv()
            spread(p)

    @pl.when(c != 0)
    def _():
        for p in range(2):
            w_col(p, 0).wait_recv()

    w = wbuf[...].reshape(nb, nb)
    own = dot(ybuf[...].reshape(rb * nb, nb), w, ((1,), (1,)))
    lead = dot(tbuf[...], w, ((1,), (1,)))
    reduced = dot(lead, own, ((1,), (1,)))
    for i in range(rb):
        flat = b_ref[pl.ds(i, sides, stride=rb), :] - reduced[:, i * nb : (i + 1) * nb]
        if i == 0:
            flat = jnp.where(r == 0, lead, flat)
        red_ref[pl.ds(i, sides, stride=rb), :] = flat
    for j in range(cb):
        across = dot(w, zbuf[j], ((1,), (0,)))
        change = dot(own, across, ((1,), (0,)))
        for i in range(rb):
            here = pl.ds(i * nb * cb + j, nb, stride=cb)
            block = a_ref[here, :] - change[i * nb : (i + 1) * nb]
            if i == 0:
                block = jnp.where(r == 0, 0.0, block)
            if j == 0:
                block = jnp.where(c == 0, own[i * nb : (i + 1) * nb], block)
            out_ref[here, :] = block

    @pl.when(root)
    def _():
        lane = lax.broadcasted_iota(jnp.int32, (nb, nb), 1)
        sub = lax.broadcasted_iota(jnp.int32, (nb, nb), 0)
        low = jnp.transpose(ubuf[...].reshape(nb, nb))
        out_ref[pl.ds(0, nb, stride=cb), :] = jnp.where(sub >= lane, low, 0.0)

    for i in range(rb):
        for b in range(bits):
            @pl.when(sends_down[b])
            def _(i=i, b=b):
                y_copy(i, b).wait_send()

    @pl.when(r < row_count - 1)
    def _():
        for j in range(cb + 1):
            z_copy(j).wait_send()

    @pl.when(root)
    def _():
        for row in range(1, row_count):
            for p in range(2):
                w_row(p, row).wait_send()

    @pl.when(c == 0)
    def _():
        for col in range(1, col_count):
            for p in range(2):
                w_col(p, col).wait_send()


def on_device(row_count, col_count, normal_matrix, right_sides):
    rb, _, nb, cb, _, _ = normal_matrix.shape
    sides = right_sides.shape[0]
    bits = max(1, (col_count - 1).bit_length())
    sizes = (row_count, col_count, rb, cb, nb, sides)
    dma = pltpu.SemaphoreType.DMA
    out, red = pl.pallas_call(
        functools.partial(kernel, sizes),
        out_shape=(
            jax.ShapeDtypeStruct((rb * nb * cb, nb), F32),
            jax.ShapeDtypeStruct((sides * rb, nb), F32),
        ),
        in_specs=[pl.BlockSpec(memory_space=pltpu.VMEM)] * 2,
        out_specs=[pl.BlockSpec(memory_space=pltpu.VMEM)] * 2,
        scratch_shapes=[
            pltpu.VMEM((rb, nb, nb), F32),
            pltpu.VMEM((cb, nb, nb), F32),
            pltpu.VMEM((sides, nb), F32),
            pltpu.VMEM((2, nb // 2, nb), F32),
            pltpu.VMEM((2, nb // 2, nb), F32),
            dma((bits, rb)),
            dma((rb,)),
            dma((cb + 1,)),
            dma((cb + 1,)),
            dma((row_count, 2)),
            dma((col_count, 2)),
            dma((2,)),
        ],
        compiler_params=pltpu.CompilerParams(
            collective_id=0, has_side_effects=True, vmem_limit_bytes=32 * 1024 * 1024
        ),
    )(normal_matrix.reshape(rb * nb * cb, nb), right_sides.reshape(sides * rb, nb))
    return out.reshape(normal_matrix.shape), red.reshape(right_sides.shape)


def solution(mesh):
    placed = (P(None, "row", None, None, "col", None), P("col", None, "row", None))
    return jax.shard_map(
        functools.partial(on_device, mesh.shape["row"], mesh.shape["col"]),
        mesh=mesh,
        in_specs=placed,
        out_specs=placed,
        check_vma=False,
    )
```

```python
import functools

import jax
import jax.numpy as jnp
from jax import lax
from jax.experimental import pallas as pl
from jax.experimental.pallas import tpu as pltpu
from jax.sharding import PartitionSpec as P

F32 = jnp.float32


def dot(a, b, dims):
    return lax.dot_general(
        a, b, (dims, ((), ())), precision=lax.Precision.HIGHEST, preferred_element_type=F32
    )


def eliminate(first, second):
    count = len(first)
    shape = first[0].shape
    sub = lax.broadcasted_iota(jnp.int32, shape, 0)
    first, second = list(first), list(second)
    for b in range(count):
        cols = [
            [jnp.broadcast_to(first[t][:, 8 * b + i : 8 * b + i + 1], shape) for i in range(8)]
            for t in range(b, count)
        ]
        e = [[None] * 8 for _ in range(8)]
        for i in range(8):
            for j in range(i + 1):
                e[j][i] = jnp.broadcast_to(cols[0][i][j : j + 1, :], shape)
        rows1 = [jnp.broadcast_to(first[b][j : j + 1, :], shape) for j in range(8)]
        rows2 = [jnp.broadcast_to(second[b][j : j + 1, :], shape) for j in range(8)]
        for k in range(8):
            scale = lax.rsqrt(e[k][k])
            low = {j: e[k][j] * scale for j in range(k + 1, 8)}
            for i in range(k + 1, 8):
                for j in range(k + 1, i + 1):
                    e[j][i] = e[j][i] - low[j] * low[i]
            rows1[k] = rows1[k] * scale
            rows2[k] = rows2[k] * scale
            for j in range(k + 1, 8):
                rows1[j] = rows1[j] - low[j] * rows1[k]
                rows2[j] = rows2[j] - low[j] * rows2[k]
            for t in range(b + 1, count):
                c = cols[t - b]
                c[k] = c[k] * scale
                for j in range(k + 1, 8):
                    c[j] = c[j] - low[j] * c[k]
                first[t] = first[t] - c[k] * rows1[k]
                second[t] = second[t] - c[k] * rows2[k]
        done1, done2 = rows1[0], rows2[0]
        for k in range(1, 8):
            done1 = jnp.where(sub == k, rows1[k], done1)
            done2 = jnp.where(sub == k, rows2[k], done2)
        first[b], second[b] = done1, done2
    return jnp.concatenate(first, axis=0), jnp.concatenate(second, axis=0)


def groups(x):
    return [x[8 * t : 8 * t + 8] for t in range(x.shape[0] // 8)]


def kernel(
    sizes, a_hbm, b_hbm, out_ref, red_ref,
    a_ref, b_ref, load, ybuf, zbuf, tbuf, wbuf, ubuf,
    ysend, yrecv, zsend, zrecv, wrow, wcol, wrecv,
):
    row_count, col_count, rb, cb, nb, sides = sizes
    half = nb // 2
    pieces = 2 * cb + 1
    r = lax.axis_index("row")
    c = lax.axis_index("col")
    bits = max(1, (col_count - 1).bit_length())
    root = (r == 0) & (c == 0)
    sends_down = [
        (lax.rem(c, 2 ** (b + 1)) == 0) & (c + 2**b < col_count) for b in range(bits)
    ]
    parent = c * 0
    for b in range(bits):
        parent = jnp.where(lax.rem(c, 2 ** (b + 1)) == 2**b, c - 2**b, parent)

    loads = (
        pltpu.make_async_copy(a_hbm, a_ref, load.at[0]),
        pltpu.make_async_copy(b_hbm, b_ref, load.at[1]),
    )
    for one in loads:
        one.start()

    barrier = pltpu.get_barrier_semaphore()

    def greet(row, col):
        pl.semaphore_signal(
            barrier, inc=1, device_id={"row": row, "col": col}, device_id_type=pl.DeviceIdType.MESH
        )

    @pl.when(c != 0)
    def _():
        greet(r, parent)
        greet(r, 0)

    @pl.when(r != 0)
    def _():
        greet(r - 1, c)

    @pl.when((r != 0) & (c == 0))
    def _():
        greet(0, 0)

    for one in loads:
        one.wait()

    @pl.when(c == 0)
    def _():
        for i in range(rb):
            ybuf[i] = a_ref[pl.ds(i * nb * cb, nb, stride=cb), :]

    @pl.when(r == 0)
    def _():
        for j in range(cb):
            zbuf[j] = a_ref[pl.ds(j, nb, stride=cb), :]
        tbuf[...] = b_ref[pl.ds(0, sides, stride=rb), :]

    targets = jnp.where(r < row_count - 1, 1, 0)
    for b in range(bits):
        targets = targets + jnp.where(sends_down[b], 1, 0)
    targets = targets + jnp.where(c == 0, col_count - 1, 0)
    targets = targets + jnp.where(root, row_count - 1, 0)

    @pl.when(targets > 0)
    def _():
        pl.semaphore_wait(barrier, targets)

    def copy(ref, send, recv, row, col):
        return pltpu.make_async_remote_copy(
            src_ref=ref,
            dst_ref=ref,
            send_sem=send,
            recv_sem=recv,
            device_id={"row": row, "col": col},
            device_id_type=pl.DeviceIdType.MESH,
        )

    def y_copy(i, b):
        return copy(ybuf.at[i], ysend.at[b, i], yrecv.at[i], r, c + 2**b)

    def z_copy(j):
        ref = zbuf.at[j // 2, pl.ds(j % 2 * half, half)] if j < 2 * cb else tbuf
        return copy(ref, zsend.at[j], zrecv.at[j], r + 1, c)

    def w_row(p, row):
        return copy(wbuf.at[p], wrow.at[row, p], wrecv.at[p], row, 0)

    def w_col(p, col):
        return copy(wbuf.at[p], wcol.at[col, p], wrecv.at[p], r, col)

    @pl.when(c == 0)
    def _():
        for i in range(rb):
            for b in reversed(range(bits)):
                @pl.when(sends_down[b])
                def _(i=i, b=b):
                    y_copy(i, b).start()

    @pl.when(r == 0)
    def _():
        for j in range(pieces):
            z_copy(j).start()

    relays = (r != 0) & (r < row_count - 1)
    inner = (c != 0) & (lax.rem(c, 2) == 0)

    def relay(j):
        z_copy(j).wait_recv()
        z_copy(j).start()

    @pl.when(relays & ~inner)
    def _():
        for j in range(pieces):
            relay(j)

    @pl.when(inner)
    def _():
        for i in range(max(rb, pieces)):
            if i < rb:
                y_copy(i, 0).wait_recv()
                for b in reversed(range(bits)):
                    @pl.when(sends_down[b])
                    def _(i=i, b=b):
                        y_copy(i, b).start()

            if i < pieces:
                @pl.when(relays)
                def _(i=i):
                    relay(i)

    def spread(p):
        for col in reversed(range(1, col_count)):
            w_col(p, col).start()

    @pl.when(root)
    def _():
        lane = lax.broadcasted_iota(jnp.int32, (half, nb), 1)
        sub = lax.broadcasted_iota(jnp.int32, (half, nb), 0)
        right = jnp.where(lane == sub + half, 1.0, 0.0).astype(F32)
        up, inv = eliminate(groups(ybuf[0, 0:half, :]), groups(right))
        wbuf[0] = pltpu.roll(inv, half, 1)
        ubuf[0] = up
        for row in reversed(range(1, row_count)):
            w_row(0, row).start()
        spread(0)
        up12 = pltpu.roll(up, half, 1)
        beside = jnp.where(lane < half, up12, inv)
        change = dot(up12, beside, ((0,), (0,)))[0:half, :]
        low_rows = pltpu.roll(ybuf[0, half:nb, :], half, 1)
        start = jnp.where(lane < half, low_rows, 0.0) - change
        up, inv = eliminate(groups(start), groups(right))
        wbuf[1] = jnp.where(lane < half, pltpu.roll(up, half, 1), inv)
        ubuf[1] = jnp.where(lane < half, 0.0, pltpu.roll(up, half, 1))
        for row in reversed(range(1, row_count)):
            w_row(1, row).start()
        spread(1)

    @pl.when((c == 0) & (r != 0))
    def _():
        for p in range(2):
            w_row(p, 0).wait_recv()
            spread(p)

    @pl.when(c != 0)
    def _():
        for p in range(2):
            w_col(p, 0).wait_recv()

    @pl.when((c != 0) & ~inner)
    def _():
        for i in range(rb):
            y_copy(i, 0).wait_recv()

    @pl.when((r != 0) & ~relays)
    def _():
        for j in range(pieces):
            z_copy(j).wait_recv()

    w = wbuf[...].reshape(nb, nb)
    own = dot(ybuf[...].reshape(rb * nb, nb), w, ((1,), (1,)))
    lead = dot(tbuf[...], w, ((1,), (1,)))
    reduced = dot(lead, own, ((1,), (1,)))
    for i in range(rb):
        flat = b_ref[pl.ds(i, sides, stride=rb), :] - reduced[:, i * nb : (i + 1) * nb]
        if i == 0:
            flat = jnp.where(r == 0, lead, flat)
        red_ref[pl.ds(i, sides, stride=rb), :] = flat
    for j in range(cb):
        across = dot(w, zbuf[j], ((1,), (0,)))
        change = dot(own, across, ((1,), (0,)))
        for i in range(rb):
            here = pl.ds(i * nb * cb + j, nb, stride=cb)
            block = a_ref[here, :] - change[i * nb : (i + 1) * nb]
            if i == 0:
                block = jnp.where(r == 0, 0.0, block)
            if j == 0:
                block = jnp.where(c == 0, own[i * nb : (i + 1) * nb], block)
            out_ref[here, :] = block

    @pl.when(root)
    def _():
        lane = lax.broadcasted_iota(jnp.int32, (nb, nb), 1)
        sub = lax.broadcasted_iota(jnp.int32, (nb, nb), 0)
        low = jnp.transpose(ubuf[...].reshape(nb, nb))
        out_ref[pl.ds(0, nb, stride=cb), :] = jnp.where(sub >= lane, low, 0.0)

    for i in range(rb):
        for b in range(bits):
            @pl.when(sends_down[b])
            def _(i=i, b=b):
                y_copy(i, b).wait_send()

    @pl.when(r < row_count - 1)
    def _():
        for j in range(pieces):
            z_copy(j).wait_send()

    @pl.when(root)
    def _():
        for row in range(1, row_count):
            for p in range(2):
                w_row(p, row).wait_send()

    @pl.when(c == 0)
    def _():
        for col in range(1, col_count):
            for p in range(2):
                w_col(p, col).wait_send()


def on_device(row_count, col_count, normal_matrix, right_sides):
    rb, _, nb, cb, _, _ = normal_matrix.shape
    sides = right_sides.shape[0]
    bits = max(1, (col_count - 1).bit_length())
    sizes = (row_count, col_count, rb, cb, nb, sides)
    dma = pltpu.SemaphoreType.DMA
    out, red = pl.pallas_call(
        functools.partial(kernel, sizes),
        out_shape=(
            jax.ShapeDtypeStruct((rb * nb * cb, nb), F32),
            jax.ShapeDtypeStruct((sides * rb, nb), F32),
        ),
        in_specs=[pl.BlockSpec(memory_space=pl.ANY)] * 2,
        out_specs=[pl.BlockSpec(memory_space=pltpu.VMEM)] * 2,
        scratch_shapes=[
            pltpu.VMEM((rb * nb * cb, nb), F32),
            pltpu.VMEM((sides * rb, nb), F32),
            dma((2,)),
            pltpu.VMEM((rb, nb, nb), F32),
            pltpu.VMEM((cb, nb, nb), F32),
            pltpu.VMEM((sides, nb), F32),
            pltpu.VMEM((2, nb // 2, nb), F32),
            pltpu.VMEM((2, nb // 2, nb), F32),
            dma((bits, rb)),
            dma((rb,)),
            dma((2 * cb + 1,)),
            dma((2 * cb + 1,)),
            dma((row_count, 2)),
            dma((col_count, 2)),
            dma((2,)),
        ],
        compiler_params=pltpu.CompilerParams(
            collective_id=0, has_side_effects=True, vmem_limit_bytes=56 * 1024 * 1024
        ),
    )(normal_matrix.reshape(rb * nb * cb, nb), right_sides.reshape(sides * rb, nb))
    return out.reshape(normal_matrix.shape), red.reshape(right_sides.shape)


def solution(mesh):
    placed = (P(None, "row", None, None, "col", None), P("col", None, "row", None))
    return jax.shard_map(
        functools.partial(on_device, mesh.shape["row"], mesh.shape["col"]),
        mesh=mesh,
        in_specs=placed,
        out_specs=placed,
        check_vma=False,
    )
```

```python
import functools

import jax
import jax.numpy as jnp
from jax import lax
from jax.experimental import pallas as pl
from jax.experimental.pallas import tpu as pltpu
from jax.sharding import PartitionSpec as P

F32 = jnp.float32


def dot(a, b, dims):
    return lax.dot_general(
        a, b, (dims, ((), ())), precision=lax.Precision.HIGHEST, preferred_element_type=F32
    )


def eliminate(first, second):
    count = len(first)
    shape = first[0].shape
    sub = lax.broadcasted_iota(jnp.int32, shape, 0)
    first, second = list(first), list(second)
    for b in range(count):
        cols = [
            [jnp.broadcast_to(first[t][:, 8 * b + i : 8 * b + i + 1], shape) for i in range(8)]
            for t in range(b, count)
        ]
        e = [[None] * 8 for _ in range(8)]
        for i in range(8):
            for j in range(i + 1):
                e[j][i] = jnp.broadcast_to(cols[0][i][j : j + 1, :], shape)
        rows1 = [jnp.broadcast_to(first[b][j : j + 1, :], shape) for j in range(8)]
        rows2 = [jnp.broadcast_to(second[b][j : j + 1, :], shape) for j in range(8)]
        for k in range(8):
            scale = lax.rsqrt(e[k][k])
            low = {j: e[k][j] * scale for j in range(k + 1, 8)}
            for i in range(k + 1, 8):
                for j in range(k + 1, i + 1):
                    e[j][i] = e[j][i] - low[j] * low[i]
            rows1[k] = rows1[k] * scale
            rows2[k] = rows2[k] * scale
            for j in range(k + 1, 8):
                rows1[j] = rows1[j] - low[j] * rows1[k]
                rows2[j] = rows2[j] - low[j] * rows2[k]
            for t in range(b + 1, count):
                c = cols[t - b]
                c[k] = c[k] * scale
                for j in range(k + 1, 8):
                    c[j] = c[j] - low[j] * c[k]
                first[t] = first[t] - c[k] * rows1[k]
                second[t] = second[t] - c[k] * rows2[k]
        done1, done2 = rows1[0], rows2[0]
        for k in range(1, 8):
            done1 = jnp.where(sub == k, rows1[k], done1)
            done2 = jnp.where(sub == k, rows2[k], done2)
        first[b], second[b] = done1, done2
    return jnp.concatenate(first, axis=0), jnp.concatenate(second, axis=0)


def groups(x):
    return [x[8 * t : 8 * t + 8] for t in range(x.shape[0] // 8)]


def tree(count):
    children = [[] for _ in range(count)]
    into = {0: 0}
    for chip in range(1, (count + 1) // 2):
        high = 1 << (chip.bit_length() - 1)
        source = chip - high
        into[chip] = into[source] if source else (chip.bit_length() - 1) % 2
        children[2 * source + into[chip]].append(2 * chip + into[chip])
    for chip in range((count + 1) // 2):
        if 2 * chip + 1 < count:
            children[2 * chip + into[chip]].append(2 * chip + 1 - into[chip])
    return children


def pick(table, index):
    value = index * 0
    for at, entry in enumerate(table):
        if entry:
            value = jnp.where(index == at, entry, value)
    return value


def kernel(
    sizes, a_hbm, b_hbm, out_ref, red_ref,
    a_ref, b_ref, load, ybuf, zbuf, tbuf, wbuf, ubuf, rest,
    ysend, yrecv, zsend, zrecv, wrow, wcol, wrecv,
):
    row_count, col_count, rb, cb, nb, sides = sizes
    half = nb // 2
    pieces = 2 * cb + 1
    r = lax.axis_index("row")
    c = lax.axis_index("col")
    children = tree(col_count)
    slots = max(len(x) for x in children)
    child = [pick([x[k] if k < len(x) else 0 for x in children], c) for k in range(slots)]
    parents = [0] * col_count
    for at, kids in enumerate(children):
        for kid in kids:
            parents[kid] = at
    parent = pick(parents, c)
    root = (r == 0) & (c == 0)
    loads = (
        pltpu.make_async_copy(a_hbm, a_ref, load.at[0]),
        pltpu.make_async_copy(b_hbm, b_ref, load.at[1]),
    )
    for one in loads:
        one.start()

    barrier = pltpu.get_barrier_semaphore()

    def greet(row, col):
        pl.semaphore_signal(
            barrier, inc=1, device_id={"row": row, "col": col}, device_id_type=pl.DeviceIdType.MESH
        )

    @pl.when(c != 0)
    def _():
        greet(r, parent)
        greet(r, 0)

    @pl.when(r != 0)
    def _():
        greet(r - 1, c)

    @pl.when((r != 0) & (c == 0))
    def _():
        greet(0, 0)

    for one in loads:
        one.wait()

    @pl.when(c == 0)
    def _():
        for i in range(rb):
            ybuf[i] = a_ref[pl.ds(i * nb * cb, nb, stride=cb), :]

    @pl.when(r == 0)
    def _():
        for j in range(cb):
            zbuf[j] = a_ref[pl.ds(j, nb, stride=cb), :]
        tbuf[...] = b_ref[pl.ds(0, sides, stride=rb), :]

    lane = lax.broadcasted_iota(jnp.int32, (half, nb), 1)
    sub = lax.broadcasted_iota(jnp.int32, (half, nb), 0)
    right = jnp.where(lane == sub + half, 1.0, 0.0).astype(F32)

    @pl.when(root)
    def _():
        up, inv = eliminate(groups(ybuf[0, 0:half, :]), groups(right))
        wbuf[0] = pltpu.roll(inv, half, 1)
        ubuf[0] = up
        up12 = pltpu.roll(up, half, 1)
        beside = jnp.where(lane < half, up12, inv)
        change = dot(up12, beside, ((0,), (0,)))[0:half, :]
        low_rows = pltpu.roll(ybuf[0, half:nb, :], half, 1)
        rest[...] = jnp.where(lane < half, low_rows, 0.0) - change

    targets = jnp.where(r < row_count - 1, 1, 0)
    for k in range(slots):
        targets = targets + jnp.where(child[k] != 0, 1, 0)
    targets = targets + jnp.where(c == 0, col_count - 1, 0)
    targets = targets + jnp.where(root, row_count - 1, 0)

    @pl.when(targets > 0)
    def _():
        pl.semaphore_wait(barrier, targets)

    def copy(ref, send, recv, row, col):
        return pltpu.make_async_remote_copy(
            src_ref=ref,
            dst_ref=ref,
            send_sem=send,
            recv_sem=recv,
            device_id={"row": row, "col": col},
            device_id_type=pl.DeviceIdType.MESH,
        )

    def y_copy(i, k):
        return copy(ybuf.at[i], ysend.at[k, i], yrecv.at[i], r, child[k])

    def z_copy(j):
        ref = zbuf.at[j // 2, pl.ds(j % 2 * half, half)] if j < 2 * cb else tbuf
        return copy(ref, zsend.at[j], zrecv.at[j], r + 1, c)

    def w_row(p, row):
        return copy(wbuf.at[p], wrow.at[row, p], wrecv.at[p], row, 0)

    def w_col(p, col):
        return copy(wbuf.at[p], wcol.at[col, p], wrecv.at[p], r, col)

    @pl.when(r == 0)
    def _():
        for j in range(pieces):
            z_copy(j).start()

    @pl.when(c == 0)
    def _():
        for i in range(rb):
            for b in range(slots):
                @pl.when(child[b] != 0)
                def _(i=i, b=b):
                    y_copy(i, b).start()

    relays = (r != 0) & (r < row_count - 1)
    inner = (c != 0) & (child[0] != 0)

    def relay(j):
        z_copy(j).wait_recv()
        z_copy(j).start()

    @pl.when(relays & ~inner)
    def _():
        for j in range(pieces):
            relay(j)

    @pl.when(inner)
    def _():
        for i in range(max(rb, pieces)):
            if i < rb:
                y_copy(i, 0).wait_recv()
                for b in range(slots):
                    @pl.when(child[b] != 0)
                    def _(i=i, b=b):
                        y_copy(i, b).start()

            if i < pieces:
                @pl.when(relays)
                def _(i=i):
                    relay(i)

    def spread(p):
        for col in reversed(range(1, col_count)):
            w_col(p, col).start()

    @pl.when(root)
    def _():
        for row in reversed(range(1, row_count)):
            w_row(0, row).start()
        spread(0)
        up, inv = eliminate(groups(rest[...]), groups(right))
        wbuf[1] = jnp.where(lane < half, pltpu.roll(up, half, 1), inv)
        for row in reversed(range(1, row_count)):
            w_row(1, row).start()
        spread(1)
        ubuf[1] = jnp.where(lane < half, 0.0, pltpu.roll(up, half, 1))

    @pl.when((c == 0) & (r != 0))
    def _():
        for p in range(2):
            w_row(p, 0).wait_recv()
            spread(p)

    @pl.when(c != 0)
    def _():
        for p in range(2):
            w_col(p, 0).wait_recv()

    @pl.when((c != 0) & ~inner)
    def _():
        for i in range(rb):
            y_copy(i, 0).wait_recv()

    @pl.when((r != 0) & ~relays)
    def _():
        for j in range(pieces):
            z_copy(j).wait_recv()

    w = wbuf[...].reshape(nb, nb)
    own = dot(ybuf[...].reshape(rb * nb, nb), w, ((1,), (1,)))
    lead = dot(tbuf[...], w, ((1,), (1,)))
    reduced = dot(lead, own, ((1,), (1,)))
    for i in range(rb):
        flat = b_ref[pl.ds(i, sides, stride=rb), :] - reduced[:, i * nb : (i + 1) * nb]
        if i == 0:
            flat = jnp.where(r == 0, lead, flat)
        red_ref[pl.ds(i, sides, stride=rb), :] = flat
    for j in range(cb):
        across = dot(w, zbuf[j], ((1,), (0,)))
        change = dot(own, across, ((1,), (0,)))
        for i in range(rb):
            here = pl.ds(i * nb * cb + j, nb, stride=cb)
            block = a_ref[here, :] - change[i * nb : (i + 1) * nb]
            if i == 0:
                block = jnp.where(r == 0, 0.0, block)
            if j == 0:
                block = jnp.where(c == 0, own[i * nb : (i + 1) * nb], block)
            out_ref[here, :] = block

    @pl.when(root)
    def _():
        lane = lax.broadcasted_iota(jnp.int32, (nb, nb), 1)
        sub = lax.broadcasted_iota(jnp.int32, (nb, nb), 0)
        low = jnp.transpose(ubuf[...].reshape(nb, nb))
        out_ref[pl.ds(0, nb, stride=cb), :] = jnp.where(sub >= lane, low, 0.0)

    for i in range(rb):
        for b in range(slots):
            @pl.when(child[b] != 0)
            def _(i=i, b=b):
                y_copy(i, b).wait_send()

    @pl.when(r < row_count - 1)
    def _():
        for j in range(pieces):
            z_copy(j).wait_send()

    @pl.when(root)
    def _():
        for row in range(1, row_count):
            for p in range(2):
                w_row(p, row).wait_send()

    @pl.when(c == 0)
    def _():
        for col in range(1, col_count):
            for p in range(2):
                w_col(p, col).wait_send()


def on_device(row_count, col_count, normal_matrix, right_sides):
    rb, _, nb, cb, _, _ = normal_matrix.shape
    sides = right_sides.shape[0]
    slots = max(len(x) for x in tree(col_count))
    sizes = (row_count, col_count, rb, cb, nb, sides)
    dma = pltpu.SemaphoreType.DMA
    out, red = pl.pallas_call(
        functools.partial(kernel, sizes),
        out_shape=(
            jax.ShapeDtypeStruct((rb * nb * cb, nb), F32),
            jax.ShapeDtypeStruct((sides * rb, nb), F32),
        ),
        in_specs=[pl.BlockSpec(memory_space=pl.ANY)] * 2,
        out_specs=[pl.BlockSpec(memory_space=pltpu.VMEM)] * 2,
        scratch_shapes=[
            pltpu.VMEM((rb * nb * cb, nb), F32),
            pltpu.VMEM((sides * rb, nb), F32),
            dma((2,)),
            pltpu.VMEM((rb, nb, nb), F32),
            pltpu.VMEM((cb, nb, nb), F32),
            pltpu.VMEM((sides, nb), F32),
            pltpu.VMEM((2, nb // 2, nb), F32),
            pltpu.VMEM((2, nb // 2, nb), F32),
            pltpu.VMEM((nb // 2, nb), F32),
            dma((slots, rb)),
            dma((rb,)),
            dma((2 * cb + 1,)),
            dma((2 * cb + 1,)),
            dma((row_count, 2)),
            dma((col_count, 2)),
            dma((2,)),
        ],
        compiler_params=pltpu.CompilerParams(
            collective_id=0, has_side_effects=True, vmem_limit_bytes=53 * 1024 * 1024 + 128 * 1024
        ),
    )(normal_matrix.reshape(rb * nb * cb, nb), right_sides.reshape(sides * rb, nb))
    return out.reshape(normal_matrix.shape), red.reshape(right_sides.shape)


def solution(mesh):
    placed = (P(None, "row", None, None, "col", None), P("col", None, "row", None))
    return jax.shard_map(
        functools.partial(on_device, mesh.shape["row"], mesh.shape["col"]),
        mesh=mesh,
        in_specs=placed,
        out_specs=placed,
        check_vma=False,
    )
```

```python
import functools

import jax
import jax.numpy as jnp
from jax import lax
from jax.experimental import pallas as pl
from jax.experimental.pallas import tpu as pltpu
from jax.sharding import PartitionSpec as P

F32 = jnp.float32


def dot(a, b, dims):
    return lax.dot_general(
        a, b, (dims, ((), ())), precision=lax.Precision.HIGHEST, preferred_element_type=F32
    )


def eliminate(first, second, early=None):
    count = len(first)
    shape = first[0].shape
    sub = lax.broadcasted_iota(jnp.int32, shape, 0)
    first, second = list(first), list(second)
    for b in range(count):
        cols = [
            [jnp.broadcast_to(first[t][:, 8 * b + i : 8 * b + i + 1], shape) for i in range(8)]
            for t in range(b, count)
        ]
        e = [[None] * 8 for _ in range(8)]
        for i in range(8):
            for j in range(i + 1):
                e[j][i] = jnp.broadcast_to(cols[0][i][j : j + 1, :], shape)
        rows1 = [jnp.broadcast_to(first[b][j : j + 1, :], shape) for j in range(8)]
        rows2 = [jnp.broadcast_to(second[b][j : j + 1, :], shape) for j in range(8)]
        for k in range(8):
            scale = lax.rsqrt(e[k][k])
            low = {j: e[k][j] * scale for j in range(k + 1, 8)}
            for i in range(k + 1, 8):
                for j in range(k + 1, i + 1):
                    e[j][i] = e[j][i] - low[j] * low[i]
            rows1[k] = rows1[k] * scale
            rows2[k] = rows2[k] * scale
            for j in range(k + 1, 8):
                rows1[j] = rows1[j] - low[j] * rows1[k]
                rows2[j] = rows2[j] - low[j] * rows2[k]
            for t in range(b + 1, count):
                c = cols[t - b]
                c[k] = c[k] * scale
                for j in range(k + 1, 8):
                    c[j] = c[j] - low[j] * c[k]
                first[t] = first[t] - c[k] * rows1[k]
                second[t] = second[t] - c[k] * rows2[k]
        done1, done2 = rows1[0], rows2[0]
        for k in range(1, 8):
            done1 = jnp.where(sub == k, rows1[k], done1)
            done2 = jnp.where(sub == k, rows2[k], done2)
        first[b], second[b] = done1, done2
        if early is not None and b == count // 2 - 1:
            early(jnp.concatenate(first[: b + 1], axis=0), jnp.concatenate(second[: b + 1], axis=0))
    return jnp.concatenate(first, axis=0), jnp.concatenate(second, axis=0)


def groups(x):
    return [x[8 * t : 8 * t + 8] for t in range(x.shape[0] // 8)]


def leader(chip):
    return (chip.bit_length() - 1) % 2 if chip and chip & (chip - 1) == 0 else 0


def tree(count):
    children = [[] for _ in range(count)]
    for chip in range(1, (count + 1) // 2):
        high = 1 << (chip.bit_length() - 1)
        low = chip & -chip
        if high == low:
            first = leader(chip)
            children[first].append(2 * chip + first)
        else:
            children[2 * (chip - high)].append(2 * chip)
            children[2 * (chip - low) + 1].append(2 * chip + 1)
    for chip in range((count + 1) // 2):
        if chip & (chip - 1) == 0:
            first = leader(chip)
            children[2 * chip + first].append(2 * chip + 1 - first)
    return children


def pick(table, index):
    value = index * 0
    for at, entry in enumerate(table):
        if entry:
            value = jnp.where(index == at, int(entry), value)
    return value


def kernel(
    sizes, a_hbm, b_hbm, out_ref, red_ref,
    a_ref, b_ref, load, ybuf, zbuf, tbuf, wbuf, ubuf, rest,
    ysend, yrecv, zsend, zrecv, wrow, wcol, wpass, wrecv,
):
    row_count, col_count, rb, cb, nb, sides = sizes
    half = nb // 2
    pieces = 2 * cb + 1
    parts = ((0, half), (half, half // 2), (half + half // 2, half // 2))
    r = lax.axis_index("row")
    c = lax.axis_index("col")
    children = tree(col_count)
    slots = max(len(x) for x in children)
    child = [pick([x[k] if k < len(x) else 0 for x in children], c) for k in range(slots)]
    parents = [0] * col_count
    for at, kids in enumerate(children):
        for kid in kids:
            parents[kid] = at
    parent = pick(parents, c)
    heads = [2 * h + leader(h) for h in range(col_count // 2)]
    partner = c + 1 - 2 * lax.rem(c, 2)
    leads = pick([at in heads for at in range(col_count)], c) == 1
    root = (r == 0) & (c == 0)
    loads = (
        pltpu.make_async_copy(a_hbm, a_ref, load.at[0]),
        pltpu.make_async_copy(b_hbm, b_ref, load.at[1]),
    )
    for one in loads:
        one.start()

    barrier = pltpu.get_barrier_semaphore()

    def greet(row, col):
        pl.semaphore_signal(
            barrier, inc=1, device_id={"row": row, "col": col}, device_id_type=pl.DeviceIdType.MESH
        )

    @pl.when(c != 0)
    def _():
        greet(r, parent)
        greet(r, jnp.where(leads, 0, partner))

    @pl.when(r != 0)
    def _():
        greet(r - 1, c)

    @pl.when((r != 0) & (c == 0))
    def _():
        greet(0, 0)

    for one in loads:
        one.wait()

    @pl.when(c == 0)
    def _():
        for i in range(rb):
            ybuf[i] = a_ref[pl.ds(i * nb * cb, nb, stride=cb), :]

    @pl.when(r == 0)
    def _():
        for j in range(cb):
            zbuf[j] = a_ref[pl.ds(j, nb, stride=cb), :]
        tbuf[...] = b_ref[pl.ds(0, sides, stride=rb), :]

    lane = lax.broadcasted_iota(jnp.int32, (half, nb), 1)
    sub = lax.broadcasted_iota(jnp.int32, (half, nb), 0)
    right = jnp.where(lane == sub + half, 1.0, 0.0).astype(F32)

    @pl.when(root)
    def _():
        up, inv = eliminate(groups(ybuf[0, 0:half, :]), groups(right))
        wbuf[pl.ds(*parts[0])] = pltpu.roll(inv, half, 1)
        ubuf[0] = up
        up12 = pltpu.roll(up, half, 1)
        beside = jnp.where(lane < half, up12, inv)
        change = dot(up12, beside, ((0,), (0,)))[0:half, :]
        low_rows = pltpu.roll(ybuf[0, half:nb, :], half, 1)
        rest[...] = jnp.where(lane < half, low_rows, 0.0) - change

    targets = jnp.where(r < row_count - 1, 1, 0)
    for k in range(slots):
        targets = targets + jnp.where(child[k] != 0, 1, 0)
    targets = targets + jnp.where(c == 0, len(heads) - 1, 0) + jnp.where(leads, 1, 0)
    targets = targets + jnp.where(root, row_count - 1, 0)

    @pl.when(targets > 0)
    def _():
        pl.semaphore_wait(barrier, targets)

    def copy(ref, send, recv, row, col):
        return pltpu.make_async_remote_copy(
            src_ref=ref,
            dst_ref=ref,
            send_sem=send,
            recv_sem=recv,
            device_id={"row": row, "col": col},
            device_id_type=pl.DeviceIdType.MESH,
        )

    def y_copy(i, k):
        return copy(ybuf.at[i], ysend.at[k, i], yrecv.at[i], r, child[k])

    def z_copy(j):
        ref = zbuf.at[j // 2, pl.ds(j % 2 * half, half)] if j < 2 * cb else tbuf
        return copy(ref, zsend.at[j], zrecv.at[j], r + 1, c)

    def w_part(p):
        return wbuf.at[pl.ds(*parts[p])]

    def w_row(p, row):
        return copy(w_part(p), wrow.at[row, p], wrecv.at[p], row, 0)

    def w_col(p, head):
        return copy(w_part(p), wcol.at[head, p], wrecv.at[p], r, heads[head])

    def w_pass(p):
        return copy(w_part(p), wpass.at[p], wrecv.at[p], r, partner)

    @pl.when(r == 0)
    def _():
        for j in range(pieces):
            z_copy(j).start()

    @pl.when(c == 0)
    def _():
        for i in range(rb):
            for b in range(slots):
                @pl.when(child[b] != 0)
                def _(i=i, b=b):
                    y_copy(i, b).start()

    relays = (r != 0) & (r < row_count - 1)
    inner = (c != 0) & (child[0] != 0)

    def relay(j):
        z_copy(j).wait_recv()
        z_copy(j).start()

    @pl.when(relays & ~inner)
    def _():
        for j in range(pieces):
            relay(j)

    @pl.when(inner)
    def _():
        for i in range(max(rb, pieces)):
            if i < rb:
                y_copy(i, 0).wait_recv()
                for b in range(slots):
                    @pl.when(child[b] != 0)
                    def _(i=i, b=b):
                        y_copy(i, b).start()

            if i < pieces:
                @pl.when(relays)
                def _(i=i):
                    relay(i)

    def spread(p):
        for head in reversed(range(1, len(heads))):
            w_col(p, head).start()
        w_pass(p).start()

    def send(p):
        for row in reversed(range(1, row_count)):
            w_row(p, row).start()
        spread(p)

    def inverse_rows(up, inv):
        wide = lax.broadcasted_iota(jnp.int32, up.shape, 1)
        return jnp.where(wide < half, pltpu.roll(up, half, 1), inv)

    @pl.when(root)
    def _():
        send(0)

        def early(up, inv):
            wbuf[pl.ds(*parts[1])] = inverse_rows(up, inv)
            send(1)

        up, inv = eliminate(groups(rest[...]), groups(right), early)
        wbuf[pl.ds(*parts[2])] = inverse_rows(up, inv)[half // 2 :]
        send(2)
        ubuf[1] = jnp.where(lane < half, 0.0, pltpu.roll(up, half, 1))

    @pl.when((c == 0) & (r != 0))
    def _():
        for p in range(3):
            w_row(p, 0).wait_recv()
            spread(p)

    @pl.when((c != 0) & leads)
    def _():
        for p in range(3):
            w_pass(p).wait_recv()
            w_pass(p).start()

    @pl.when(~leads)
    def _():
        for p in range(3):
            w_pass(p).wait_recv()

    @pl.when((c != 0) & ~inner)
    def _():
        for i in range(rb):
            y_copy(i, 0).wait_recv()

    @pl.when((r != 0) & ~relays)
    def _():
        for j in range(pieces):
            z_copy(j).wait_recv()

    w = wbuf[...]
    own = dot(ybuf[...].reshape(rb * nb, nb), w, ((1,), (1,)))
    lead = dot(tbuf[...], w, ((1,), (1,)))
    reduced = dot(lead, own, ((1,), (1,)))
    for i in range(rb):
        flat = b_ref[pl.ds(i, sides, stride=rb), :] - reduced[:, i * nb : (i + 1) * nb]
        if i == 0:
            flat = jnp.where(r == 0, lead, flat)
        red_ref[pl.ds(i, sides, stride=rb), :] = flat
    for j in range(cb):
        across = dot(w, zbuf[j], ((1,), (0,)))
        change = dot(own, across, ((1,), (0,)))
        for i in range(rb):
            here = pl.ds(i * nb * cb + j, nb, stride=cb)
            block = a_ref[here, :] - change[i * nb : (i + 1) * nb]
            if i == 0:
                block = jnp.where(r == 0, 0.0, block)
            if j == 0:
                block = jnp.where(c == 0, own[i * nb : (i + 1) * nb], block)
            out_ref[here, :] = block

    @pl.when(root)
    def _():
        lane = lax.broadcasted_iota(jnp.int32, (nb, nb), 1)
        sub = lax.broadcasted_iota(jnp.int32, (nb, nb), 0)
        low = jnp.transpose(ubuf[...].reshape(nb, nb))
        out_ref[pl.ds(0, nb, stride=cb), :] = jnp.where(sub >= lane, low, 0.0)

    for i in range(rb):
        for b in range(slots):
            @pl.when(child[b] != 0)
            def _(i=i, b=b):
                y_copy(i, b).wait_send()

    @pl.when(r < row_count - 1)
    def _():
        for j in range(pieces):
            z_copy(j).wait_send()

    @pl.when(root)
    def _():
        for row in range(1, row_count):
            for p in range(3):
                w_row(p, row).wait_send()

    @pl.when(c == 0)
    def _():
        for head in range(1, len(heads)):
            for p in range(3):
                w_col(p, head).wait_send()

    @pl.when(leads)
    def _():
        for p in range(3):
            w_pass(p).wait_send()


def on_device(row_count, col_count, normal_matrix, right_sides):
    rb, _, nb, cb, _, _ = normal_matrix.shape
    sides = right_sides.shape[0]
    slots = max(len(x) for x in tree(col_count))
    sizes = (row_count, col_count, rb, cb, nb, sides)
    dma = pltpu.SemaphoreType.DMA
    out, red = pl.pallas_call(
        functools.partial(kernel, sizes),
        out_shape=(
            jax.ShapeDtypeStruct((rb * nb * cb, nb), F32),
            jax.ShapeDtypeStruct((sides * rb, nb), F32),
        ),
        in_specs=[pl.BlockSpec(memory_space=pl.ANY)] * 2,
        out_specs=[pl.BlockSpec(memory_space=pltpu.VMEM)] * 2,
        scratch_shapes=[
            pltpu.VMEM((rb * nb * cb, nb), F32),
            pltpu.VMEM((sides * rb, nb), F32),
            dma((2,)),
            pltpu.VMEM((rb, nb, nb), F32),
            pltpu.VMEM((cb, nb, nb), F32),
            pltpu.VMEM((sides, nb), F32),
            pltpu.VMEM((nb, nb), F32),
            pltpu.VMEM((2, nb // 2, nb), F32),
            pltpu.VMEM((nb // 2, nb), F32),
            dma((slots, rb)),
            dma((rb,)),
            dma((2 * cb + 1,)),
            dma((2 * cb + 1,)),
            dma((row_count, 3)),
            dma((col_count // 2, 3)),
            dma((3,)),
            dma((3,)),
        ],
        compiler_params=pltpu.CompilerParams(
            collective_id=0, has_side_effects=True, vmem_limit_bytes=53 * 1024 * 1024 + 128 * 1024
        ),
    )(normal_matrix.reshape(rb * nb * cb, nb), right_sides.reshape(sides * rb, nb))
    return out.reshape(normal_matrix.shape), red.reshape(right_sides.shape)


def solution(mesh):
    placed = (P(None, "row", None, None, "col", None), P("col", None, "row", None))
    return jax.shard_map(
        functools.partial(on_device, mesh.shape["row"], mesh.shape["col"]),
        mesh=mesh,
        in_specs=placed,
        out_specs=placed,
        check_vma=False,
    )
```

```python
import functools

import jax
import jax.numpy as jnp
from jax import lax
from jax.experimental import pallas as pl
from jax.experimental.pallas import tpu as pltpu
from jax.sharding import PartitionSpec as P

F32 = jnp.float32


def dot(a, b, dims):
    return lax.dot_general(
        a, b, (dims, ((), ())), precision=lax.Precision.HIGHEST, preferred_element_type=F32
    )


def eliminate(first, second, early=None):
    count = len(first)
    shape = first[0].shape
    sub = lax.broadcasted_iota(jnp.int32, shape, 0)
    first, second = list(first), list(second)
    for b in range(count):
        cols = [
            [jnp.broadcast_to(first[t][:, 8 * b + i : 8 * b + i + 1], shape) for i in range(8)]
            for t in range(b, count)
        ]
        e = [[None] * 8 for _ in range(8)]
        for i in range(8):
            for j in range(i + 1):
                e[j][i] = jnp.broadcast_to(cols[0][i][j : j + 1, :], shape)
        rows1 = [jnp.broadcast_to(first[b][j : j + 1, :], shape) for j in range(8)]
        rows2 = [jnp.broadcast_to(second[b][j : j + 1, :], shape) for j in range(8)]
        for k in range(8):
            scale = lax.rsqrt(e[k][k])
            low = {j: e[k][j] * scale for j in range(k + 1, 8)}
            for i in range(k + 1, 8):
                for j in range(k + 1, i + 1):
                    e[j][i] = e[j][i] - low[j] * low[i]
            rows1[k] = rows1[k] * scale
            rows2[k] = rows2[k] * scale
            for j in range(k + 1, 8):
                rows1[j] = rows1[j] - low[j] * rows1[k]
                rows2[j] = rows2[j] - low[j] * rows2[k]
            for t in range(b + 1, count):
                c = cols[t - b]
                c[k] = c[k] * scale
                for j in range(k + 1, 8):
                    c[j] = c[j] - low[j] * c[k]
                first[t] = first[t] - c[k] * rows1[k]
                second[t] = second[t] - c[k] * rows2[k]
        done1, done2 = rows1[0], rows2[0]
        for k in range(1, 8):
            done1 = jnp.where(sub == k, rows1[k], done1)
            done2 = jnp.where(sub == k, rows2[k], done2)
        first[b], second[b] = done1, done2
        if early is not None and b == count // 2 - 1:
            early(jnp.concatenate(first[: b + 1], axis=0), jnp.concatenate(second[: b + 1], axis=0))
    return jnp.concatenate(first, axis=0), jnp.concatenate(second, axis=0)


def groups(x):
    return [x[8 * t : 8 * t + 8] for t in range(x.shape[0] // 8)]


def leader(chip):
    return (chip.bit_length() - 1) % 2 if chip and chip & (chip - 1) == 0 else 0


def tree(count):
    children = [[] for _ in range(count)]
    for chip in range(1, (count + 1) // 2):
        high = 1 << (chip.bit_length() - 1)
        low = chip & -chip
        if high == low:
            first = leader(chip)
            children[first].append(2 * chip + first)
        else:
            children[2 * (chip - high)].append(2 * chip)
            children[2 * (chip - low) + 1].append(2 * chip + 1)
    for chip in range((count + 1) // 2):
        if chip & (chip - 1) == 0:
            first = leader(chip)
            children[2 * chip + first].append(2 * chip + 1 - first)
    return children


def pick(table, index):
    value = index * 0
    for at, entry in enumerate(table):
        if entry:
            value = jnp.where(index == at, int(entry), value)
    return value


def kernel(
    sizes, a_hbm, b_hbm, out_ref, red_ref,
    a_ref, b_ref, load, ybuf, zbuf, tbuf, wbuf, ubuf, rest,
    ysend, yrecv, zsend, zrecv, wrow, wcol, wpass, wrecv,
):
    row_count, col_count, rb, cb, nb, sides = sizes
    half = nb // 2
    pieces = 2 * cb + 1
    parts = ((0, half), (half, half // 2), (half + half // 2, half // 2))
    r = lax.axis_index("row")
    c = lax.axis_index("col")
    children = tree(col_count)
    slots = max(len(x) for x in children)
    child = [pick([x[k] if k < len(x) else 0 for x in children], c) for k in range(slots)]
    parents = [0] * col_count
    for at, kids in enumerate(children):
        for kid in kids:
            parents[kid] = at
    parent = pick(parents, c)
    heads = [2 * h + leader(h) for h in range(col_count // 2)]
    partner = c + 1 - 2 * lax.rem(c, 2)
    leads = pick([at in heads for at in range(col_count)], c) == 1
    root = (r == 0) & (c == 0)
    loads = (
        pltpu.make_async_copy(a_hbm, a_ref, load.at[0]),
        pltpu.make_async_copy(b_hbm, b_ref, load.at[1]),
    )
    for one in loads:
        one.start()

    barrier = pltpu.get_barrier_semaphore()

    def greet(row, col):
        pl.semaphore_signal(
            barrier, inc=1, device_id={"row": row, "col": col}, device_id_type=pl.DeviceIdType.MESH
        )

    @pl.when(c != 0)
    def _():
        greet(r, parent)
        greet(r, jnp.where(leads, 0, partner))

    @pl.when(r != 0)
    def _():
        greet(r - 1, c)

    @pl.when((r != 0) & (c == 0))
    def _():
        greet(0, 0)

    for one in loads:
        one.wait()

    @pl.when(c == 0)
    def _():
        for i in range(rb):
            ybuf[i] = a_ref[pl.ds(i * nb * cb, nb, stride=cb), :]

    @pl.when(r == 0)
    def _():
        for j in range(cb):
            zbuf[j] = a_ref[pl.ds(j, nb, stride=cb), :]
        tbuf[...] = b_ref[pl.ds(0, sides, stride=rb), :]

    lane = lax.broadcasted_iota(jnp.int32, (half, nb), 1)
    sub = lax.broadcasted_iota(jnp.int32, (half, nb), 0)
    right = jnp.where(lane == sub + half, 1.0, 0.0).astype(F32)

    @pl.when(root)
    def _():
        up, inv = eliminate(groups(ybuf[0, 0:half, :]), groups(right))
        wbuf[pl.ds(*parts[0])] = pltpu.roll(inv, half, 1)
        ubuf[0] = up
        up12 = pltpu.roll(up, half, 1)
        beside = jnp.where(lane < half, up12, inv)
        change = dot(up12, beside, ((0,), (0,)))[0:half, :]
        low_rows = pltpu.roll(ybuf[0, half:nb, :], half, 1)
        rest[...] = jnp.where(lane < half, low_rows, 0.0) - change

    targets = jnp.where(r < row_count - 1, 1, 0)
    for k in range(slots):
        targets = targets + jnp.where(child[k] != 0, 1, 0)
    targets = targets + jnp.where(c == 0, len(heads) - 1, 0) + jnp.where(leads, 1, 0)
    targets = targets + jnp.where(root, row_count - 1, 0)

    @pl.when(targets > 0)
    def _():
        pl.semaphore_wait(barrier, targets)

    def copy(ref, send, recv, row, col):
        return pltpu.make_async_remote_copy(
            src_ref=ref,
            dst_ref=ref,
            send_sem=send,
            recv_sem=recv,
            device_id={"row": row, "col": col},
            device_id_type=pl.DeviceIdType.MESH,
        )

    def y_copy(i, k):
        return copy(ybuf.at[i], ysend.at[k, i], yrecv.at[i], r, child[k])

    def z_copy(j):
        ref = zbuf.at[j // 2, pl.ds(j % 2 * half, half)] if j < 2 * cb else tbuf
        return copy(ref, zsend.at[j], zrecv.at[j], r + 1, c)

    def w_part(p):
        return wbuf.at[pl.ds(*parts[p])]

    def w_row(p, row):
        return copy(w_part(p), wrow.at[row, p], wrecv.at[p], row, 0)

    def w_col(p, head):
        return copy(w_part(p), wcol.at[head, p], wrecv.at[p], r, heads[head])

    def w_pass(p):
        return copy(w_part(p), wpass.at[p], wrecv.at[p], r, partner)

    @pl.when(r == 0)
    def _():
        for j in range(pieces):
            z_copy(j).start()

    @pl.when(c == 0)
    def _():
        for i in range(rb):
            for b in range(slots):
                @pl.when(child[b] != 0)
                def _(i=i, b=b):
                    y_copy(i, b).start()

    relays = (r != 0) & (r < row_count - 1)
    inner = (c != 0) & (child[0] != 0)

    def relay(j):
        z_copy(j).wait_recv()
        z_copy(j).start()

    @pl.when(relays & ~inner)
    def _():
        for j in range(pieces):
            relay(j)

    @pl.when(inner)
    def _():
        for i in range(max(rb, pieces + 2)):
            if i < rb:
                y_copy(i, 0).wait_recv()
                for b in range(slots):
                    @pl.when(child[b] != 0)
                    def _(i=i, b=b):
                        y_copy(i, b).start()

            if 2 <= i < pieces + 2:
                @pl.when(relays)
                def _(i=i):
                    relay(i - 2)

    def spread(p):
        for head in reversed(range(1, len(heads))):
            w_col(p, head).start()
        w_pass(p).start()

    def send(p):
        for row in reversed(range(1, row_count)):
            w_row(p, row).start()
        spread(p)

    def inverse_rows(up, inv):
        wide = lax.broadcasted_iota(jnp.int32, up.shape, 1)
        return jnp.where(wide < half, pltpu.roll(up, half, 1), inv)

    @pl.when(root)
    def _():
        send(0)

        def early(up, inv):
            wbuf[pl.ds(*parts[1])] = inverse_rows(up, inv)
            send(1)

        up, inv = eliminate(groups(rest[...]), groups(right), early)
        wbuf[pl.ds(*parts[2])] = inverse_rows(up, inv)[half // 2 :]
        send(2)
        ubuf[1] = jnp.where(lane < half, 0.0, pltpu.roll(up, half, 1))

    @pl.when((c == 0) & (r != 0))
    def _():
        for p in range(3):
            w_row(p, 0).wait_recv()
            spread(p)

    @pl.when((c != 0) & leads)
    def _():
        for p in range(3):
            w_pass(p).wait_recv()
            w_pass(p).start()

    @pl.when(~leads)
    def _():
        for p in range(3):
            w_pass(p).wait_recv()

    @pl.when((c != 0) & ~inner)
    def _():
        for i in range(rb):
            y_copy(i, 0).wait_recv()

    @pl.when((r != 0) & ~relays)
    def _():
        for j in range(pieces):
            z_copy(j).wait_recv()

    w = wbuf[...]
    own = dot(ybuf[...].reshape(rb * nb, nb), w, ((1,), (1,)))
    lead = dot(tbuf[...], w, ((1,), (1,)))
    reduced = dot(lead, own, ((1,), (1,)))
    for i in range(rb):
        flat = b_ref[pl.ds(i, sides, stride=rb), :] - reduced[:, i * nb : (i + 1) * nb]
        if i == 0:
            flat = jnp.where(r == 0, lead, flat)
        red_ref[pl.ds(i, sides, stride=rb), :] = flat
    across = dot(w, jnp.concatenate([zbuf[j] for j in range(cb)], axis=1), ((1,), (0,)))
    change = dot(own, across, ((1,), (0,)))
    for j in range(cb):
        for i in range(rb):
            here = pl.ds(i * nb * cb + j, nb, stride=cb)
            block = a_ref[here, :] - change[i * nb : (i + 1) * nb, j * nb : (j + 1) * nb]
            if i == 0:
                block = jnp.where(r == 0, 0.0, block)
            if j == 0:
                block = jnp.where(c == 0, own[i * nb : (i + 1) * nb], block)
            out_ref[here, :] = block

    @pl.when(root)
    def _():
        lane = lax.broadcasted_iota(jnp.int32, (nb, nb), 1)
        sub = lax.broadcasted_iota(jnp.int32, (nb, nb), 0)
        low = jnp.transpose(ubuf[...].reshape(nb, nb))
        out_ref[pl.ds(0, nb, stride=cb), :] = jnp.where(sub >= lane, low, 0.0)

    for i in range(rb):
        for b in range(slots):
            @pl.when(child[b] != 0)
            def _(i=i, b=b):
                y_copy(i, b).wait_send()

    @pl.when(r < row_count - 1)
    def _():
        for j in range(pieces):
            z_copy(j).wait_send()

    @pl.when(root)
    def _():
        for row in range(1, row_count):
            for p in range(3):
                w_row(p, row).wait_send()

    @pl.when(c == 0)
    def _():
        for head in range(1, len(heads)):
            for p in range(3):
                w_col(p, head).wait_send()

    @pl.when(leads)
    def _():
        for p in range(3):
            w_pass(p).wait_send()


def on_device(row_count, col_count, normal_matrix, right_sides):
    rb, _, nb, cb, _, _ = normal_matrix.shape
    sides = right_sides.shape[0]
    slots = max(len(x) for x in tree(col_count))
    sizes = (row_count, col_count, rb, cb, nb, sides)
    dma = pltpu.SemaphoreType.DMA
    out, red = pl.pallas_call(
        functools.partial(kernel, sizes),
        out_shape=(
            jax.ShapeDtypeStruct((rb * nb * cb, nb), F32),
            jax.ShapeDtypeStruct((sides * rb, nb), F32),
        ),
        in_specs=[pl.BlockSpec(memory_space=pl.ANY)] * 2,
        out_specs=[pl.BlockSpec(memory_space=pltpu.VMEM)] * 2,
        scratch_shapes=[
            pltpu.VMEM((rb * nb * cb, nb), F32),
            pltpu.VMEM((sides * rb, nb), F32),
            dma((2,)),
            pltpu.VMEM((rb, nb, nb), F32),
            pltpu.VMEM((cb, nb, nb), F32),
            pltpu.VMEM((sides, nb), F32),
            pltpu.VMEM((nb, nb), F32),
            pltpu.VMEM((2, nb // 2, nb), F32),
            pltpu.VMEM((nb // 2, nb), F32),
            dma((slots, rb)),
            dma((rb,)),
            dma((2 * cb + 1,)),
            dma((2 * cb + 1,)),
            dma((row_count, 3)),
            dma((col_count // 2, 3)),
            dma((3,)),
            dma((3,)),
        ],
        compiler_params=pltpu.CompilerParams(
            collective_id=0, has_side_effects=True, vmem_limit_bytes=53 * 1024 * 1024 + 128 * 1024
        ),
    )(normal_matrix.reshape(rb * nb * cb, nb), right_sides.reshape(sides * rb, nb))
    return out.reshape(normal_matrix.shape), red.reshape(right_sides.shape)


def solution(mesh):
    placed = (P(None, "row", None, None, "col", None), P("col", None, "row", None))
    return jax.shard_map(
        functools.partial(on_device, mesh.shape["row"], mesh.shape["col"]),
        mesh=mesh,
        in_specs=placed,
        out_specs=placed,
        check_vma=False,
    )
```

```python
import functools

import jax
import jax.numpy as jnp
from jax import lax
from jax.experimental import pallas as pl
from jax.experimental.pallas import tpu as pltpu
from jax.sharding import PartitionSpec as P

F32 = jnp.float32


def dot(a, b, dims):
    return lax.dot_general(
        a, b, (dims, ((), ())), precision=lax.Precision.HIGHEST, preferred_element_type=F32
    )


def eliminate(first, second, early=None):
    count = len(first)
    shape = first[0].shape
    sub = lax.broadcasted_iota(jnp.int32, shape, 0)
    first, second = list(first), list(second)
    for b in range(count):
        cols = [
            [jnp.broadcast_to(first[t][:, 8 * b + i : 8 * b + i + 1], shape) for i in range(8)]
            for t in range(b, count)
        ]
        e = [[None] * 8 for _ in range(8)]
        for i in range(8):
            for j in range(i + 1):
                e[j][i] = jnp.broadcast_to(cols[0][i][j : j + 1, :], shape)
        rows1 = [jnp.broadcast_to(first[b][j : j + 1, :], shape) for j in range(8)]
        rows2 = [jnp.broadcast_to(second[b][j : j + 1, :], shape) for j in range(8)]
        for k in range(8):
            scale = lax.rsqrt(e[k][k])
            low = {j: e[k][j] * scale for j in range(k + 1, 8)}
            for i in range(k + 1, 8):
                for j in range(k + 1, i + 1):
                    e[j][i] = e[j][i] - low[j] * low[i]
            rows1[k] = rows1[k] * scale
            rows2[k] = rows2[k] * scale
            for j in range(k + 1, 8):
                rows1[j] = rows1[j] - low[j] * rows1[k]
                rows2[j] = rows2[j] - low[j] * rows2[k]
            for t in range(b + 1, count):
                c = cols[t - b]
                c[k] = c[k] * scale
                for j in range(k + 1, 8):
                    c[j] = c[j] - low[j] * c[k]
                first[t] = first[t] - c[k] * rows1[k]
                second[t] = second[t] - c[k] * rows2[k]
        done1, done2 = rows1[0], rows2[0]
        for k in range(1, 8):
            done1 = jnp.where(sub == k, rows1[k], done1)
            done2 = jnp.where(sub == k, rows2[k], done2)
        first[b], second[b] = done1, done2
        if early is not None and b == count // 2 - 1:
            early(jnp.concatenate(first[: b + 1], axis=0), jnp.concatenate(second[: b + 1], axis=0))
    return jnp.concatenate(first, axis=0), jnp.concatenate(second, axis=0)


def groups(x):
    return [x[8 * t : 8 * t + 8] for t in range(x.shape[0] // 8)]


def leader(chip):
    return (chip.bit_length() - 1) % 2 if chip and chip & (chip - 1) == 0 else 0


def tree(count):
    children = [[] for _ in range(count)]
    for chip in range(1, (count + 1) // 2):
        high = 1 << (chip.bit_length() - 1)
        low = chip & -chip
        if high == low:
            first = leader(chip)
            children[first].append(2 * chip + first)
        else:
            children[2 * (chip - high)].append(2 * chip)
            children[2 * (chip - low) + 1].append(2 * chip + 1)
    for chip in range((count + 1) // 2):
        if chip & (chip - 1) == 0:
            first = leader(chip)
            children[2 * chip + first].append(2 * chip + 1 - first)
    return children


def pick(table, index):
    value = index * 0
    for at, entry in enumerate(table):
        if entry:
            value = jnp.where(index == at, int(entry), value)
    return value


def kernel(
    sizes, a_hbm, b_hbm, out_ref, red_ref,
    a_ref, b_ref, load, ybuf, zbuf, tbuf, wbuf, ubuf, rest,
    ysend, yrecv, zsend, zrecv, wrow, wcol, wpass, wrecv,
):
    row_count, col_count, rb, cb, nb, sides = sizes
    half = nb // 2
    pieces = 2 * cb + 1
    parts = ((0, half), (half, half // 2), (half + half // 2, half // 2))
    r = lax.axis_index("row")
    c = lax.axis_index("col")
    children = tree(col_count)
    slots = max(len(x) for x in children)
    child = [pick([x[k] if k < len(x) else 0 for x in children], c) for k in range(slots)]
    parents = [0] * col_count
    for at, kids in enumerate(children):
        for kid in kids:
            parents[kid] = at
    parent = pick(parents, c)
    heads = [2 * h + leader(h) for h in range(col_count // 2)]
    partner = c + 1 - 2 * lax.rem(c, 2)
    leads = pick([at in heads for at in range(col_count)], c) == 1
    root = (r == 0) & (c == 0)
    loads = (
        pltpu.make_async_copy(a_hbm, a_ref, load.at[0]),
        pltpu.make_async_copy(b_hbm, b_ref, load.at[1]),
    )
    for one in loads:
        one.start()

    barrier = pltpu.get_barrier_semaphore()

    def greet(row, col):
        pl.semaphore_signal(
            barrier, inc=1, device_id={"row": row, "col": col}, device_id_type=pl.DeviceIdType.MESH
        )

    @pl.when(c != 0)
    def _():
        greet(r, parent)
        greet(r, jnp.where(leads, 0, partner))

    @pl.when(r != 0)
    def _():
        greet(r - 1, c)

    @pl.when((r != 0) & (c == 0))
    def _():
        greet(0, 0)

    for one in loads:
        one.wait()

    @pl.when(c == 0)
    def _():
        for i in range(rb):
            ybuf[i] = a_ref[pl.ds(i * nb * cb, nb, stride=cb), :]

    @pl.when(r == 0)
    def _():
        for j in range(cb):
            zbuf[j] = a_ref[pl.ds(j, nb, stride=cb), :]
        tbuf[...] = b_ref[pl.ds(0, sides, stride=rb), :]

    lane = lax.broadcasted_iota(jnp.int32, (half, nb), 1)
    sub = lax.broadcasted_iota(jnp.int32, (half, nb), 0)
    right = jnp.where(lane == sub + half, 1.0, 0.0).astype(F32)

    @pl.when(root)
    def _():
        up, inv = eliminate(groups(ybuf[0, 0:half, :]), groups(right))
        wbuf[pl.ds(*parts[0])] = pltpu.roll(inv, half, 1)
        ubuf[0] = up
        up12 = pltpu.roll(up, half, 1)
        beside = jnp.where(lane < half, up12, inv)
        change = dot(up12, beside, ((0,), (0,)))[0:half, :]
        low_rows = pltpu.roll(ybuf[0, half:nb, :], half, 1)
        rest[...] = jnp.where(lane < half, low_rows, 0.0) - change

    targets = jnp.where(r < row_count - 1, 1, 0)
    for k in range(slots):
        targets = targets + jnp.where(child[k] != 0, 1, 0)
    targets = targets + jnp.where(c == 0, len(heads) - 1, 0) + jnp.where(leads, 1, 0)
    targets = targets + jnp.where(root, row_count - 1, 0)

    @pl.when(targets > 0)
    def _():
        pl.semaphore_wait(barrier, targets)

    def copy(ref, send, recv, row, col):
        return pltpu.make_async_remote_copy(
            src_ref=ref,
            dst_ref=ref,
            send_sem=send,
            recv_sem=recv,
            device_id={"row": row, "col": col},
            device_id_type=pl.DeviceIdType.MESH,
        )

    def y_copy(i, k):
        return copy(ybuf.at[i], ysend.at[k, i], yrecv.at[i], r, child[k])

    def z_copy(j):
        ref = zbuf.at[j // 2, pl.ds(j % 2 * half, half)] if j < 2 * cb else tbuf
        return copy(ref, zsend.at[j], zrecv.at[j], r + 1, c)

    def w_part(p):
        return wbuf.at[pl.ds(*parts[p])]

    def w_row(p, row):
        return copy(w_part(p), wrow.at[row, p], wrecv.at[p], row, 0)

    def w_col(p, head):
        return copy(w_part(p), wcol.at[head, p], wrecv.at[p], r, heads[head])

    def w_pass(p):
        return copy(w_part(p), wpass.at[p], wrecv.at[p], r, partner)

    @pl.when(r == 0)
    def _():
        for j in range(pieces):
            z_copy(j).start()

    @pl.when(c == 0)
    def _():
        for i in range(rb):
            for b in range(slots):
                @pl.when(child[b] != 0)
                def _(i=i, b=b):
                    y_copy(i, b).start()

    relays = (r != 0) & (r < row_count - 1)
    late = relays & (r >= 2) & leads
    ahead = relays & ~late
    inner = (c != 0) & (child[0] != 0)

    def relay(j):
        z_copy(j).wait_recv()
        z_copy(j).start()

    @pl.when(ahead & ~inner)
    def _():
        for j in range(pieces):
            relay(j)

    @pl.when(inner)
    def _():
        for i in range(max(rb, pieces + 2)):
            if i < rb:
                y_copy(i, 0).wait_recv()
                for b in range(slots):
                    @pl.when(child[b] != 0)
                    def _(i=i, b=b):
                        y_copy(i, b).start()

            if 2 <= i < pieces + 2:
                @pl.when(ahead)
                def _(i=i):
                    relay(i - 2)

    def spread(p):
        for head in reversed(range(1, len(heads))):
            w_col(p, head).start()
        w_pass(p).start()

    def send(p):
        for row in reversed(range(1, row_count)):
            w_row(p, row).start()
        spread(p)

    def inverse_rows(up, inv):
        wide = lax.broadcasted_iota(jnp.int32, up.shape, 1)
        return jnp.where(wide < half, pltpu.roll(up, half, 1), inv)

    @pl.when(root)
    def _():
        send(0)

        def early(up, inv):
            wbuf[pl.ds(*parts[1])] = inverse_rows(up, inv)
            send(1)

        up, inv = eliminate(groups(rest[...]), groups(right), early)
        wbuf[pl.ds(*parts[2])] = inverse_rows(up, inv)[half // 2 :]
        send(2)
        ubuf[1] = jnp.where(lane < half, 0.0, pltpu.roll(up, half, 1))

    @pl.when((c == 0) & (r != 0))
    def _():
        for p in range(3):
            w_row(p, 0).wait_recv()
            spread(p)

    @pl.when((c != 0) & leads)
    def _():
        for p in range(3):
            w_pass(p).wait_recv()
            w_pass(p).start()

    @pl.when(~leads)
    def _():
        for p in range(3):
            w_pass(p).wait_recv()

    @pl.when(late)
    def _():
        for j in range(pieces):
            relay(j)

    @pl.when((c != 0) & ~inner)
    def _():
        for i in range(rb):
            y_copy(i, 0).wait_recv()

    @pl.when((r != 0) & ~relays)
    def _():
        for j in range(pieces):
            z_copy(j).wait_recv()

    w = wbuf[...]
    own = dot(ybuf[...].reshape(rb * nb, nb), w, ((1,), (1,)))
    lead = dot(tbuf[...], w, ((1,), (1,)))
    reduced = dot(lead, own, ((1,), (1,)))
    for i in range(rb):
        flat = b_ref[pl.ds(i, sides, stride=rb), :] - reduced[:, i * nb : (i + 1) * nb]
        if i == 0:
            flat = jnp.where(r == 0, lead, flat)
        red_ref[pl.ds(i, sides, stride=rb), :] = flat
    across = dot(w, jnp.concatenate([zbuf[j] for j in range(cb)], axis=1), ((1,), (0,)))
    change = dot(own, across, ((1,), (0,)))
    for j in range(cb):
        for i in range(rb):
            here = pl.ds(i * nb * cb + j, nb, stride=cb)
            block = a_ref[here, :] - change[i * nb : (i + 1) * nb, j * nb : (j + 1) * nb]
            if i == 0:
                block = jnp.where(r == 0, 0.0, block)
            if j == 0:
                block = jnp.where(c == 0, own[i * nb : (i + 1) * nb], block)
            out_ref[here, :] = block

    @pl.when(root)
    def _():
        lane = lax.broadcasted_iota(jnp.int32, (nb, nb), 1)
        sub = lax.broadcasted_iota(jnp.int32, (nb, nb), 0)
        low = jnp.transpose(ubuf[...].reshape(nb, nb))
        out_ref[pl.ds(0, nb, stride=cb), :] = jnp.where(sub >= lane, low, 0.0)

    for i in range(rb):
        for b in range(slots):
            @pl.when(child[b] != 0)
            def _(i=i, b=b):
                y_copy(i, b).wait_send()

    @pl.when(r < row_count - 1)
    def _():
        for j in range(pieces):
            z_copy(j).wait_send()

    @pl.when(root)
    def _():
        for row in range(1, row_count):
            for p in range(3):
                w_row(p, row).wait_send()

    @pl.when(c == 0)
    def _():
        for head in range(1, len(heads)):
            for p in range(3):
                w_col(p, head).wait_send()

    @pl.when(leads)
    def _():
        for p in range(3):
            w_pass(p).wait_send()


def on_device(row_count, col_count, normal_matrix, right_sides):
    rb, _, nb, cb, _, _ = normal_matrix.shape
    sides = right_sides.shape[0]
    slots = max(len(x) for x in tree(col_count))
    sizes = (row_count, col_count, rb, cb, nb, sides)
    dma = pltpu.SemaphoreType.DMA
    out, red = pl.pallas_call(
        functools.partial(kernel, sizes),
        out_shape=(
            jax.ShapeDtypeStruct((rb * nb * cb, nb), F32),
            jax.ShapeDtypeStruct((sides * rb, nb), F32),
        ),
        in_specs=[pl.BlockSpec(memory_space=pl.ANY)] * 2,
        out_specs=[pl.BlockSpec(memory_space=pltpu.VMEM)] * 2,
        scratch_shapes=[
            pltpu.VMEM((rb * nb * cb, nb), F32),
            pltpu.VMEM((sides * rb, nb), F32),
            dma((2,)),
            pltpu.VMEM((rb, nb, nb), F32),
            pltpu.VMEM((cb, nb, nb), F32),
            pltpu.VMEM((sides, nb), F32),
            pltpu.VMEM((nb, nb), F32),
            pltpu.VMEM((2, nb // 2, nb), F32),
            pltpu.VMEM((nb // 2, nb), F32),
            dma((slots, rb)),
            dma((rb,)),
            dma((2 * cb + 1,)),
            dma((2 * cb + 1,)),
            dma((row_count, 3)),
            dma((col_count // 2, 3)),
            dma((3,)),
            dma((3,)),
        ],
        compiler_params=pltpu.CompilerParams(
            collective_id=0, has_side_effects=True, vmem_limit_bytes=53 * 1024 * 1024 + 128 * 1024
        ),
    )(normal_matrix.reshape(rb * nb * cb, nb), right_sides.reshape(sides * rb, nb))
    return out.reshape(normal_matrix.shape), red.reshape(right_sides.shape)


def solution(mesh):
    placed = (P(None, "row", None, None, "col", None), P("col", None, "row", None))
    return jax.shard_map(
        functools.partial(on_device, mesh.shape["row"], mesh.shape["col"]),
        mesh=mesh,
        in_specs=placed,
        out_specs=placed,
        check_vma=False,
    )
```
